1024 devices in a mesh: lat: 16 (over y, core), lon: 64 (over x, z).
Axes of the slice: x: 8, y: 8, z: 8, core: 2. Of those that a mesh axis runs over, the one named last changes fastest.
Arguments:
- layer_temp: float32 [256, 35, 8192], P('lat', None, 'lon'), may hold values from -20 to -2
- ice_depth_per_class: float32 [256, 5, 8192], P('lat', None, 'lon'), may hold values from 0.5 to 3
- ice_area: float32 [256, 5, 8192], P('lat', None, 'lon'), may hold values from 0.05 to 0.2
- surf_temp: float32 [256, 8192], P('lat', 'lon'), may hold values from -30 to -2
- seawater_thermal_input: float32 [256, 8192], P('lat', 'lon'), may hold values from 0 to 0.3
- velocity: float32 [2, 256, 8192], P(None, 'lat', 'lon'), may hold values from -1.2 to 1.2
- stress: float32 [3, 256, 8192], P(None, 'lat', 'lon'), may hold values from -3 to 3
- wind_stress: float32 [2, 256, 8192], P(None, 'lat', 'lon'), may hold values from -1.8 to 1.8
- current: float32 [2, 256, 8192], P(None, 'lat', 'lon'), may hold values from -1.8 to 1.8
- land_mask: int32 [256, 8192], P('lat', 'lon'), may hold values 0 or 1
- ice_mask: int32 [64, 256], P('lon', 'lat'), may hold values from 0 to 1, as said below
- band_index: int32 [256], P('lat'), may hold values from 0 to 63, as said below
Outputs:
- temp_after: float32 [256, 35, 8192], P('lat', None, 'lon')
- thick_after: float32 [256, 5, 8192], P('lat', None, 'lon')
- velocity_after: float32 [2, 256, 8192], P(None, 'lat', 'lon')
- stress_after: float32 [3, 256, 8192], P(None, 'lat', 'lon')
- zonal_volume: float32 [64], P('lat')
The draws below stay inside these ranges and needn't reach their ends.
Inputs may be any that keep to these rules, and one draw needn't show every extreme that they name: `ice_mask`: for each lat index, the strips of all devices with that index include at most 448 ice-covered strips and more than (6) times the number of lon devices; among these devices one has all its 16 strips ice-covered. `band_index`: every band holds 1 to 7 rows, which lie next to one another; one band holds exactly 7.
All inputs are finite; a program needn't handle non-finite values. No bound on the sum of `land_mask` on one device may be relied on, other than what follows from the above.
Results may differ from the reference program's by a relative error of at most 0.00002.
Values sent between devices are 32-bit elements; how exact they have to be, the bound alone decides.
No kernel may reach another device: no remote copies, remote signals or barrier semaphores. Data moves between devices by JAX's collectives and lax.ppermute only.
A program may use at most 32 MiB of HBM per device.

```python
import math
import jax
import jax.numpy as jnp
from jax import lax

DEPTH_CLASSES = 5
VERTICAL_LEVELS = 7
ROWS_DEV = 16
COLS_DEV = 128
SUBCYCLES = 3
SWEEPS = 2
ICE_DEV = 7
GRID_ROWS = 256
GRID_COLS = 8192
BANDS = 64
N_LAT = 16
N_LON = 64


def ice_row_group(group_key):
    count_key, full_key, shuffle_key = jax.random.split(group_key, 3)
    strip_total = N_LON * ROWS_DEV
    ice_total = N_LON * (ICE_DEV - 1) + jax.random.randint(count_key, (), 1, N_LON + 1)
    full_device = jax.random.randint(full_key, (), 0, N_LON)
    shuffled = jax.random.permutation(shuffle_key, strip_total)
    owner_lon = jnp.arange(strip_total, dtype=jnp.int32) // ROWS_DEV
    priority = jnp.where(owner_lon == full_device, shuffled - strip_total, shuffled)
    position = jnp.argsort(jnp.argsort(priority, stable=True), stable=True)
    return (position < ice_total).astype(jnp.int32).reshape(N_LON, ROWS_DEV)


def draw_ice_mask(key, part):
    row_keys = jax.random.split(jax.random.fold_in(key, 7), N_LAT)
    grouped = jax.vmap(ice_row_group)(row_keys)
    return jnp.transpose(grouped, (1, 0, 2)).reshape(N_LON, N_LAT * ROWS_DEV)


def draw_band_index(key, part):
    shift_key, pick_key, pair_key = jax.random.split(jax.random.fold_in(key, 11), 3)
    base_rows = ROWS_DEV // 4
    pair_count = BANDS // 2
    moved = jax.random.randint(shift_key, (pair_count,), -(base_rows - 1), base_rows)
    chosen_pair = jax.random.randint(pick_key, (), 0, pair_count)
    moved = jnp.where(jnp.arange(pair_count, dtype=jnp.int32) == chosen_pair, base_rows - 1, moved)
    shuffled = jax.random.permutation(pair_key, BANDS).astype(jnp.int32)
    place = jnp.argsort(shuffled, stable=True).astype(jnp.int32)
    pair_of_band = place // 2
    side = place % 2
    band_rows = (base_rows + moved[pair_of_band] * (1 - 2 * side)).astype(jnp.int32)
    band_ends = jnp.cumsum(band_rows)
    row_ids = jnp.arange(GRID_ROWS, dtype=jnp.int32)
    upward = jnp.sum((band_ends[None, :] <= row_ids[:, None]).astype(jnp.int32), axis=1)
    return ((upward + BANDS // 2) % BANDS).astype(jnp.int32)


def place_ends(entries, key, low, top_value):
    shape = entries.shape
    index_at = [jax.random.randint(jax.random.fold_in(key, axis), (), 0, shape[axis]) for axis in range(len(shape))]
    entries = entries.at[tuple(index_at)].set(low)
    longest = shape.index(max(shape))
    index_at[longest] = (index_at[longest] + 1) % shape[longest]
    return entries.at[tuple(index_at)].set(top_value)


def shard_levels(stream_key, dims, cuts, least, largest):
    def one(axis_at, parts):
        steps = jax.random.uniform(jax.random.fold_in(jax.random.fold_in(stream_key, 6), axis_at), (parts,), jnp.float32, least / len(cuts), largest / len(cuts))
        return jnp.repeat(jnp.exp(steps), dims[axis_at] // parts).reshape((-1,) + (1,) * (len(dims) - axis_at - 1))

    level = one(*cuts[0])
    for cut in cuts[1:]:
        level = level * one(*cut)
    return level


def gaussian(rng, shape, spread, reach, cuts=(), kind=jnp.bfloat16):
    result = spread * jax.random.normal(rng, shape, jnp.float32)
    if cuts:
        result = result * shard_levels(rng, shape, cuts, -0.22, 0.18)
    return jnp.clip(result, -reach, reach).astype(kind)


def setup_inputs(seed: int = 0) -> dict:
    streams_of = jax.random.split(jax.random.key(seed), 13)
    layer_temp = jnp.clip(-20.0 + 18.0 * jax.random.uniform(streams_of[0], (GRID_ROWS, DEPTH_CLASSES * VERTICAL_LEVELS, GRID_COLS), jnp.float32) ** shard_levels(streams_of[0], (GRID_ROWS, DEPTH_CLASSES * VERTICAL_LEVELS, GRID_COLS), ((0, 16), (2, 64)), -0.2, 0.2), -20.0, -2.0)
    ice_depth_per_class = jnp.clip(jnp.exp(math.log(3.0) - 1.7917595 * jax.random.uniform(streams_of[1], (GRID_ROWS, DEPTH_CLASSES, GRID_COLS), jnp.float32) ** shard_levels(streams_of[1], (GRID_ROWS, DEPTH_CLASSES, GRID_COLS), ((0, 16), (2, 64)), -0.2, 0.2)), 0.5, 3.0)
    ice_area = jnp.clip(jnp.exp(math.log(0.2) - 1.3862944 * jax.random.uniform(streams_of[2], (GRID_ROWS, DEPTH_CLASSES, GRID_COLS), jnp.float32) ** shard_levels(streams_of[2], (GRID_ROWS, DEPTH_CLASSES, GRID_COLS), ((0, 16), (2, 64)), -0.2, 0.2)), 0.05, 0.2)
    surf_temp = jnp.clip(-30.0 + 28.0 * jax.random.uniform(streams_of[3], (GRID_ROWS, GRID_COLS), jnp.float32) ** shard_levels(streams_of[3], (GRID_ROWS, GRID_COLS), ((0, 16), (1, 64)), -0.2, 0.2), -30.0, -2.0)
    seawater_thermal_input = jnp.clip(0.3 * jax.random.uniform(streams_of[4], (GRID_ROWS, GRID_COLS), jnp.float32) ** shard_levels(streams_of[4], (GRID_ROWS, GRID_COLS), ((0, 16), (1, 64)), -0.2, 0.2), 0.0, 0.3)
    velocity = gaussian(streams_of[5], (2, GRID_ROWS, GRID_COLS), 0.2, 1.2, ((1, 16), (2, 64)), jnp.float32)
    stress = gaussian(streams_of[6], (3, GRID_ROWS, GRID_COLS), 0.5, 3.0, ((1, 16), (2, 64)), jnp.float32)
    wind_stress = gaussian(streams_of[7], (2, GRID_ROWS, GRID_COLS), 0.3, 1.8, ((1, 16), (2, 64)), jnp.float32)
    current = gaussian(streams_of[8], (2, GRID_ROWS, GRID_COLS), 0.3, 1.8, ((1, 16), (2, 64)), jnp.float32)
    land_mask = place_ends((jax.random.randint(streams_of[9], (GRID_ROWS, GRID_COLS), 0, 10) < 9).astype(jnp.int32), jax.random.fold_in(streams_of[9], 1), 0, 1)
    ice_mask = draw_ice_mask(jax.random.fold_in(streams_of[12], 71), 0)
    band_index = draw_band_index(jax.random.fold_in(streams_of[12], 71), 0)
    return dict(layer_temp=layer_temp, ice_depth_per_class=ice_depth_per_class, ice_area=ice_area, surf_temp=surf_temp, seawater_thermal_input=seawater_thermal_input, velocity=velocity, stress=stress, wind_stress=wind_stress, current=current, land_mask=land_mask, ice_mask=ice_mask, band_index=band_index)


FREEZE_POINT = -1.8
BASE_CONDUCT = 2.03
SALT_CONDUCT = 0.416
CONDUCT_SCALE = 1.0
GROWTH_RATE = 0.02
STRENGTH_SCALE = 1.0
STRENGTH_DECAY = 5.0
ELLIPSE_SQUARE = 4.0
STRAIN_FLOOR = 0.0025
STRESS_RELAX = 0.5
MOMENTUM_STEP = 0.5
WATER_DRAG = 1.0

def update_vertical_cell(thermal_state_levels, ice_depth_per_class, upper_interface_state, seawater_thermal_input):
    first_extent = thermal_state_levels.shape[:-2]
    vertical_cell_group = thermal_state_levels.shape[-1]
    vertical_levels_state = thermal_state_levels.reshape(first_extent + (DEPTH_CLASSES, VERTICAL_LEVELS, vertical_cell_group))
    before = [vertical_levels_state[..., layer_at, :] for layer_at in range(VERTICAL_LEVELS)]
    surface_row = upper_interface_state[..., None, :]
    scaled = CONDUCT_SCALE / (ice_depth_per_class * ice_depth_per_class)
    repeated_pass = before
    for picard_turn in range(SWEEPS):
        conductance = [BASE_CONDUCT + SALT_CONDUCT / guessed for guessed in repeated_pass]
        couplings = [scaled * conductance[0]]
        for layer_at in range(1, VERTICAL_LEVELS):
            couplings.append(scaled * 0.5 * (conductance[layer_at - 1] + conductance[layer_at]))
        couplings.append(scaled * conductance[VERTICAL_LEVELS - 1])
        upper_ratio = []
        eliminated = []
        for layer_at in range(VERTICAL_LEVELS):
            source_term = before[layer_at]
            divisor = 1.0 + couplings[layer_at] + couplings[layer_at + 1]
            if layer_at == 0:
                source_term = source_term + couplings[0] * surface_row
            else:
                divisor = divisor - couplings[layer_at] * upper_ratio[layer_at - 1]
                source_term = source_term + couplings[layer_at] * eliminated[layer_at - 1]
            if layer_at == VERTICAL_LEVELS - 1:
                source_term = source_term + couplings[VERTICAL_LEVELS] * FREEZE_POINT
            upper_ratio.append(couplings[layer_at + 1] / divisor)
            eliminated.append(source_term / divisor)
        solved = list(eliminated)
        for layer_at in range(VERTICAL_LEVELS - 2, -1, -1):
            solved[layer_at] = eliminated[layer_at] + upper_ratio[layer_at] * solved[layer_at + 1]
        repeated_pass = solved
    bottom = repeated_pass[VERTICAL_LEVELS - 1]
    regrown = ice_depth_per_class + GROWTH_RATE * (BASE_CONDUCT + SALT_CONDUCT / bottom) * (FREEZE_POINT - bottom) / ice_depth_per_class - seawater_thermal_input[..., None, :]
    updated_vertical_cells = jnp.stack(repeated_pass, axis=-2).reshape(thermal_state_levels.shape)
    return (updated_vertical_cells, regrown)

def pad_rim(field, margin):
    wrapped = jnp.concatenate([field[..., -margin:], field, field[..., :margin]], axis=-1)
    spacing = [(0, 0)] * (field.ndim - 2) + [(margin, margin), (0, 0)]
    return jnp.pad(wrapped, spacing)

def stress_update(zonal_field, meridional_field, previous, strength):
    zonal_east = (zonal_field[1:-1, 2:] - zonal_field[1:-1, :-2]) * 0.5
    zonal_north = (zonal_field[2:, 1:-1] - zonal_field[:-2, 1:-1]) * 0.5
    meridional_east = (meridional_field[1:-1, 2:] - meridional_field[1:-1, :-2]) * 0.5
    meridional_north = (meridional_field[2:, 1:-1] - meridional_field[:-2, 1:-1]) * 0.5
    divergence = zonal_east + meridional_north
    tension = zonal_east - meridional_north
    shearing = zonal_north + meridional_east
    deformation = jnp.sqrt(divergence * divergence + (tension * tension + shearing * shearing) / ELLIPSE_SQUARE + STRAIN_FLOOR)
    viscous = strength / deformation
    bulk_new = (previous[0] + STRESS_RELAX * viscous * (divergence - deformation)) / (1.0 + STRESS_RELAX)
    tension_new = (previous[1] + STRESS_RELAX * viscous * tension / ELLIPSE_SQUARE) / (1.0 + STRESS_RELAX)
    shear_new = (previous[2] + STRESS_RELAX * viscous * shearing / (2.0 * ELLIPSE_SQUARE)) / (1.0 + STRESS_RELAX)
    return jnp.stack([bulk_new, tension_new, shear_new])

def force_update(padded, velocity, ice_mass, wind_stress, current, wet_cells):
    normal_east = 0.5 * (padded[0] + padded[1])
    normal_north = 0.5 * (padded[0] - padded[1])
    shear_stress = padded[2]
    push_east = (normal_east[1:-1, 2:] - normal_east[1:-1, :-2]) * 0.5 + (shear_stress[2:, 1:-1] - shear_stress[:-2, 1:-1]) * 0.5
    push_north = (shear_stress[1:-1, 2:] - shear_stress[1:-1, :-2]) * 0.5 + (normal_north[2:, 1:-1] - normal_north[:-2, 1:-1]) * 0.5
    pushes = jnp.stack([push_east, push_north])
    moved = velocity + MOMENTUM_STEP * (pushes / ice_mass + wind_stress + WATER_DRAG * current)
    return wet_cells * moved / (1.0 + MOMENTUM_STEP * WATER_DRAG)

def one_block(pieces):
    return update_vertical_cell(pieces[0], pieces[1], pieces[2], pieces[3])

def reference(layer_temp, ice_depth_per_class, ice_area, surf_temp, seawater_thermal_input, velocity, stress, wind_stress, current, land_mask, ice_mask, band_index):
    strip_ice = jnp.repeat(jnp.transpose(ice_mask), COLS_DEV, axis=1) == 1
    blocks = (layer_temp.reshape(N_LAT, ROWS_DEV, DEPTH_CLASSES * VERTICAL_LEVELS, GRID_COLS), ice_depth_per_class.reshape(N_LAT, ROWS_DEV, DEPTH_CLASSES, GRID_COLS), surf_temp.reshape(N_LAT, ROWS_DEV, GRID_COLS), seawater_thermal_input.reshape(N_LAT, ROWS_DEV, GRID_COLS))
    stepped_temp, stepped_thick = lax.map(one_block, blocks)
    stepped_temp = stepped_temp.reshape(layer_temp.shape)
    stepped_thick = stepped_thick.reshape(ice_depth_per_class.shape)
    temp_after = jnp.where(strip_ice[:, None, :], stepped_temp, layer_temp)
    thick_after = jnp.where(strip_ice[:, None, :], stepped_thick, ice_depth_per_class)
    volume_start = lax.optimization_barrier(jnp.sum(ice_area * ice_depth_per_class, axis=1))
    coverage = lax.optimization_barrier(jnp.sum(ice_area, axis=1))
    strength = STRENGTH_SCALE * volume_start * jnp.exp(-STRENGTH_DECAY * (1.0 - coverage))
    ice_mass = 1.0 + volume_start
    wet_cells = land_mask.astype(jnp.float32)
    moving = velocity
    stresses = stress
    for subcycle in range(SUBCYCLES):
        padded_velocity = pad_rim(moving, 1)
        stresses = stress_update(padded_velocity[0], padded_velocity[1], stresses, strength)
        moving = force_update(pad_rim(stresses, 1), moving, ice_mass, wind_stress, current, wet_cells)
    volume_after = lax.optimization_barrier(jnp.sum(ice_area * thick_after, axis=1))
    row_total = lax.optimization_barrier(jnp.sum(volume_after, axis=1))
    members = (band_index[:, None] == jnp.arange(BANDS, dtype=jnp.int32)[None, :]).astype(jnp.float32)
    band_sum = lax.optimization_barrier(jnp.sum(members * row_total[:, None], axis=0))
    band_cells = lax.optimization_barrier(jnp.sum(members, axis=0)) * GRID_COLS
    zonal_volume = band_sum / band_cells
    return (temp_after, thick_after, moving, stresses, zonal_volume)
```

```python
import jax
import jax.numpy as jnp
from jax import lax
from jax.sharding import PartitionSpec as P

DEPTH_CLASSES = 5
VERTICAL_LEVELS = 7
SUBCYCLES = 3
SWEEPS = 2
BANDS_DEV = 4

FREEZE_POINT = -1.8
BASE_CONDUCT = 2.03
SALT_CONDUCT = 0.416
GROWTH_RATE = 0.02
STRENGTH_DECAY = 5.0
STRAIN_FLOOR = 0.0025

WIDTHS = (6, 6, 5, 5, 5, 5, 4, 4, 4, 4)


def columns_step(temp, depth, surf):
    scaled = 1.0 / (depth * depth)
    half = scaled * 0.5
    guess = temp
    for sweep in range(SWEEPS):
        conduct = [BASE_CONDUCT + SALT_CONDUCT / g for g in guess]
        coupling = [scaled * conduct[0]]
        for k in range(1, VERTICAL_LEVELS):
            coupling.append(half * (conduct[k - 1] + conduct[k]))
        coupling.append(scaled * conduct[VERTICAL_LEVELS - 1])
        ratio, passed = [], []
        for k in range(VERTICAL_LEVELS):
            source = temp[k]
            divisor = 1.0 + coupling[k] + coupling[k + 1]
            if k == 0:
                source = source + coupling[0] * surf
            else:
                divisor = divisor - coupling[k] * ratio[k - 1]
                source = source + coupling[k] * passed[k - 1]
            if k == VERTICAL_LEVELS - 1:
                source = source + coupling[VERTICAL_LEVELS] * FREEZE_POINT
            inverse = 1.0 / divisor
            ratio.append(coupling[k + 1] * inverse)
            passed.append(source * inverse)
        solved = list(passed)
        for k in range(VERTICAL_LEVELS - 2, -1, -1):
            solved[k] = passed[k] + ratio[k] * solved[k + 1]
        guess = solved
    return guess


def rows_exchange(planes):
    n = lax.axis_size("lat")
    up = [(i, i + 1) for i in range(n - 1)]
    down = [(i + 1, i) for i in range(n - 1)]
    last = jnp.concatenate([p[-w:] for p, w in zip(planes, WIDTHS)], axis=0)
    first = jnp.concatenate([p[:w] for p, w in zip(planes, WIDTHS)], axis=0)
    return lax.ppermute(last, "lat", up), lax.ppermute(first, "lat", down)


def rows_joined(planes, before, after):
    out, at = [], 0
    for p, w in zip(planes, WIDTHS):
        out.append(jnp.concatenate([before[at : at + w], p, after[at : at + w]], axis=0))
        at += w
    return out


def evened(p, rows):
    gap = (rows - p.shape[0]) // 2
    return jnp.pad(p, ((gap, gap), (0, 0))) if gap else p


def cols_exchange(planes):
    n = lax.axis_size("lon")
    right = [(i, (i + 1) % n) for i in range(n)]
    left = [((i + 1) % n, i) for i in range(n)]
    rows = planes[0].shape[0]
    last = jnp.concatenate([evened(p[:, -w:], rows) for p, w in zip(planes, WIDTHS)], axis=1)
    first = jnp.concatenate([evened(p[:, :w], rows) for p, w in zip(planes, WIDTHS)], axis=1)
    return lax.ppermute(last, "lon", right), lax.ppermute(first, "lon", left)


def cols_joined(planes, before, after):
    out, at = [], 0
    for p, w in zip(planes, WIDTHS):
        gap = (before.shape[0] - p.shape[0]) // 2
        rows = slice(gap, gap + p.shape[0])
        out.append(
            jnp.concatenate([before[rows, at : at + w], p, after[rows, at : at + w]], axis=1)
        )
        at += w
    return out


def trim(p, n):
    return p[n:-n, n:-n] if n else p


def east(p):
    return (p[1:-1, 2:] - p[1:-1, :-2]) * 0.5


def north(p):
    return (p[2:, 1:-1] - p[:-2, 1:-1]) * 0.5


def subcycles(planes):
    u, v, s1, s2, s12, strength, a, b, cx, cy = planes
    third = 1.0 / 1.5
    for step in range(SUBCYCLES):
        left = 2 * (SUBCYCLES - 1 - step)
        ue, un, ve, vn = east(u), north(u), east(v), north(v)
        divergence, tension, shearing = ue + vn, ue - vn, un + ve
        square = (
            divergence * divergence
            + (tension * tension + shearing * shearing) * 0.25
            + STRAIN_FLOOR
        )
        inverse = lax.rsqrt(square)
        pull = trim(strength, 2 * step) * inverse
        s1 = (s1 + 0.5 * pull * (divergence - square * inverse)) * third
        s2 = (s2 + 0.125 * pull * tension) * third
        s12 = (s12 + 0.0625 * pull * shearing) * third
        n11, n22 = 0.5 * (s1 + s2), 0.5 * (s1 - s2)
        px, py = east(n11) + north(s12), east(s12) + north(n22)
        n = 2 * step
        u = trim(a, n) * trim(u, 2) + trim(b, n) * px + trim(cx, n)
        v = trim(a, n) * trim(v, 2) + trim(b, n) * py + trim(cy, n)
        if step < SUBCYCLES - 1:
            s1, s2, s12 = trim(s1, 2), trim(s2, 2), trim(s12, 2)
        else:
            s1, s2, s12 = trim(s1, 1), trim(s2, 1), trim(s12, 1)
    return jnp.stack([u, v]), jnp.stack([s1, s2, s12])


def local(
    layer_temp,
    ice_depth_per_class,
    ice_area,
    surf_temp,
    seawater_thermal_input,
    velocity,
    stress,
    wind_stress,
    current,
    land_mask,
    ice_mask,
    band_index,
):
    rows, _, cols = layer_temp.shape
    lat_size, lon_size = lax.axis_size("lat"), lax.axis_size("lon")
    strip_ice = (ice_mask[0] == 1)[:, None, None]

    layers = layer_temp.reshape(rows, DEPTH_CLASSES, VERTICAL_LEVELS, cols)
    temp = [layers[:, :, k] for k in range(VERTICAL_LEVELS)]
    solved = columns_step(temp, ice_depth_per_class, surf_temp[:, None])
    bottom = solved[-1]
    regrown = (
        ice_depth_per_class
        + GROWTH_RATE * (BASE_CONDUCT + SALT_CONDUCT / bottom) * (FREEZE_POINT - bottom)
        / ice_depth_per_class
        - seawater_thermal_input[:, None]
    )
    thick_after = jnp.where(strip_ice, regrown, ice_depth_per_class)
    temp_after = jnp.where(
        strip_ice, jnp.stack(solved, axis=2).reshape(layer_temp.shape), layer_temp
    )

    row_total = jnp.sum(ice_area * thick_after, axis=(1, 2))
    bands = jnp.arange(BANDS_DEV * lat_size, dtype=jnp.int32)
    members = (band_index[:, None] == bands[None, :]).astype(jnp.float32)
    part_sum = jnp.sum(members * row_total[:, None], axis=0).reshape(lat_size, 1, BANDS_DEV)
    part_rows = jnp.sum(members, axis=0).reshape(lat_size, 1, BANDS_DEV)
    parts = jnp.concatenate([part_sum, part_rows], axis=2)

    volume_start = jnp.sum(ice_area * ice_depth_per_class, axis=1)
    coverage = jnp.sum(ice_area, axis=1)
    strength = volume_start * jnp.exp(-STRENGTH_DECAY * (1.0 - coverage))
    a = land_mask.astype(jnp.float32) * (1.0 / 1.5)
    half = 0.5 * a
    b = half / (1.0 + volume_start)
    push = wind_stress + current
    planes = [
        velocity[0], velocity[1], stress[0], stress[1], stress[2],
        strength, a, b, half * push[0], half * push[1],
    ]

    parts, planes = lax.optimization_barrier((parts, planes))
    arrived = lax.all_to_all(parts, "lat", 0, 0, tiled=True)
    before, after = rows_exchange(planes)
    total = jnp.sum(arrived, axis=(0, 1))
    share = total[:BANDS_DEV] / (total[BANDS_DEV:] * float(cols * lon_size))
    spread = jnp.broadcast_to(share[None, None], (lon_size, 1, BANDS_DEV))
    spread, before, after = lax.optimization_barrier((spread, before, after))
    shares = lax.all_to_all(spread, "lon", 0, 0, tiled=True)
    planes = rows_joined(planes, before, after)
    before, after = cols_exchange(planes)
    planes = cols_joined(planes, before, after)
    moving, stresses = subcycles(planes)
    zonal_volume = jnp.sum(shares, axis=(0, 1))
    return (temp_after, thick_after, moving, stresses, zonal_volume)


def solution(mesh):
    return jax.shard_map(
        local,
        mesh=mesh,
        in_specs=(
            P("lat", None, "lon"),
            P("lat", None, "lon"),
            P("lat", None, "lon"),
            P("lat", "lon"),
            P("lat", "lon"),
            P(None, "lat", "lon"),
            P(None, "lat", "lon"),
            P(None, "lat", "lon"),
            P(None, "lat", "lon"),
            P("lat", "lon"),
            P("lon", "lat"),
            P("lat"),
        ),
        out_specs=(
            P("lat", None, "lon"),
            P("lat", None, "lon"),
            P(None, "lat", "lon"),
            P(None, "lat", "lon"),
            P("lat"),
        ),
        check_vma=False,
    )
```

```python
import jax
import jax.numpy as jnp
from jax import lax
from jax.experimental import pallas as pl
from jax.experimental.pallas import tpu as pltpu
from jax.sharding import PartitionSpec as P

DEPTH_CLASSES = 5
VERTICAL_LEVELS = 7
SUBCYCLES = 3
SWEEPS = 2
BANDS_DEV = 4

FREEZE_POINT = -1.8
BASE_CONDUCT = 2.03
SALT_CONDUCT = 0.416
GROWTH_RATE = 0.02
STRENGTH_DECAY = 5.0
STRAIN_FLOOR = 0.0025

PLANES = 10
EDGE = 8
WIDTH = 6
THIRD = 1.0 / 1.5


def columns_step(temp, depth, surf):
    scaled = 1.0 / (depth * depth)
    half = scaled * 0.5
    guess = temp
    for sweep in range(SWEEPS):
        conduct = [BASE_CONDUCT + SALT_CONDUCT / g for g in guess]
        coupling = [scaled * conduct[0]]
        for k in range(1, VERTICAL_LEVELS):
            coupling.append(half * (conduct[k - 1] + conduct[k]))
        coupling.append(scaled * conduct[VERTICAL_LEVELS - 1])
        ratio, passed = [], []
        for k in range(VERTICAL_LEVELS):
            source = temp[k]
            divisor = 1.0 + coupling[k] + coupling[k + 1]
            if k == 0:
                source = source + coupling[0] * surf
            else:
                divisor = divisor - coupling[k] * ratio[k - 1]
                source = source + coupling[k] * passed[k - 1]
            if k == VERTICAL_LEVELS - 1:
                source = source + coupling[VERTICAL_LEVELS] * FREEZE_POINT
            inverse = 1.0 / divisor
            ratio.append(coupling[k + 1] * inverse)
            passed.append(source * inverse)
        solved = list(passed)
        for k in range(VERTICAL_LEVELS - 2, -1, -1):
            solved[k] = passed[k] + ratio[k] * solved[k + 1]
        guess = solved
    return guess


def columns_kernel(*refs):
    n = 12
    given, outs, here, sems = refs[:n], refs[n : n + 5], refs[n + 5 : n + 5 + n], refs[-1]
    copies = [pltpu.make_async_copy(a, b, sems.at[i]) for i, (a, b) in enumerate(zip(given, here))]
    for copy in copies:
        copy.start()
    for copy in copies:
        copy.wait()
    columns_body(*here, *outs)


def columns_body(
    temp_ref, depth_ref, area_ref, surf_ref, sea_ref, velocity_ref, stress_ref, wind_ref, current_ref,
    land_ref, ice_ref, band_ref, temp_out, thick_out, parts_out, first_out, last_out,
):
    rows = surf_ref.shape[0]
    depth, area = depth_ref[...], area_ref[...]

    volume = jnp.sum(area * depth, axis=0)
    coverage = jnp.sum(area, axis=0)
    a = land_ref[...].astype(jnp.float32) * THIRD
    half = 0.5 * a
    planes = (
        velocity_ref[0], velocity_ref[1], stress_ref[0], stress_ref[1], stress_ref[2],
        volume * jnp.exp(-STRENGTH_DECAY * (1.0 - coverage)),
        a, half / (1.0 + volume),
        half * (wind_ref[0] + current_ref[0]), half * (wind_ref[1] + current_ref[1]),
    )
    for f, plane in enumerate(planes):
        first_out[f] = plane[:EDGE]
        last_out[f] = plane[rows - EDGE :]

    temp = [
        jnp.stack([temp_ref[c * VERTICAL_LEVELS + k] for c in range(DEPTH_CLASSES)])
        for k in range(VERTICAL_LEVELS)
    ]
    solved = columns_step(temp, depth, surf_ref[...][None])
    bottom = solved[-1]
    regrown = (
        depth
        + GROWTH_RATE * (BASE_CONDUCT + SALT_CONDUCT / bottom) * (FREEZE_POINT - bottom) / depth
        - sea_ref[...][None]
    )
    square = (rows, rows)
    eye = lax.broadcasted_iota(jnp.int32, square, 0) == lax.broadcasted_iota(jnp.int32, square, 1)
    ice = jnp.broadcast_to(ice_ref[...].astype(jnp.float32), square)
    ice = jnp.sum(jnp.where(eye, ice, 0.0), axis=1, keepdims=True)
    ice = jnp.broadcast_to(ice, surf_ref.shape) == 1.0
    thick = [jnp.where(ice, regrown[c], depth[c]) for c in range(DEPTH_CLASSES)]
    after = area[0] * thick[0]
    for c in range(1, DEPTH_CLASSES):
        after = after + area[c] * thick[c]
    for c in range(DEPTH_CLASSES):
        thick_out[c] = thick[c]
        for k in range(VERTICAL_LEVELS):
            temp_out[c * VERTICAL_LEVELS + k] = jnp.where(ice, solved[k][c], temp[k][c])

    owners, _, entries = parts_out.shape
    total = jnp.broadcast_to(jnp.sum(after, axis=1, keepdims=True), (rows, entries))
    entry = lax.broadcasted_iota(jnp.int32, (owners, entries), 1)
    band = BANDS_DEV * lax.broadcasted_iota(jnp.int32, (owners, entries), 0) + entry % BANDS_DEV
    parts = jnp.zeros((owners, entries), jnp.float32)
    for r in range(rows):
        value = jnp.where(entry < BANDS_DEV, jnp.broadcast_to(total[r : r + 1], parts.shape), 1.0)
        parts = parts + jnp.where(band == band_ref[r], value, 0.0)
    parts_out[...] = parts[:, None, :]


def window(f, first_ref, last_ref, before_ref, after_ref):
    return jnp.concatenate([first_ref[f], last_ref[f], after_ref[f], before_ref[f]], axis=0)


def lanes_of(shape):
    return lax.broadcasted_iota(jnp.int32, shape, 1)


def pack_kernel(first_ref, last_ref, before_ref, after_ref, right_out, left_out):
    cols = right_out.shape[1]
    lanes = lanes_of(right_out.shape)
    right = jnp.zeros(right_out.shape, jnp.float32)
    left = jnp.zeros(right_out.shape, jnp.float32)
    for f in range(PLANES):
        plane = window(f, first_ref, last_ref, before_ref, after_ref)
        at = f * WIDTH
        here = (lanes >= at) & (lanes < at + WIDTH)
        right = jnp.where(here, pltpu.roll(plane, (at + WIDTH) % cols, 1), right)
        left = jnp.where(here, pltpu.roll(plane, at, 1) if at else plane, left)
    right_out[...] = right
    left_out[...] = left


def east(p):
    n = p.shape[1]
    return (pltpu.roll(p, n - 1, 1) - pltpu.roll(p, 1, 1)) * 0.5


def north(p):
    n = p.shape[0]
    return (pltpu.roll(p, n - 1, 0) - pltpu.roll(p, 1, 0)) * 0.5


def subcycles_kernel(
    first_ref, last_ref, before_ref, after_ref, west_ref, east_ref, velocity_out, stress_out
):
    rows, cols = velocity_out.shape[1:]
    west, onward = west_ref[...], east_ref[...]
    lanes = lanes_of(west.shape)
    fields = []
    for f in range(PLANES):
        at = f * WIDTH
        near = pltpu.roll(onward, cols - at, 1) if at else onward
        far = pltpu.roll(west, cols - WIDTH - at, 1)
        side = jnp.where(lanes < WIDTH, near, jnp.where(lanes >= cols - WIDTH, far, 0.0))
        plane = window(f, first_ref, last_ref, before_ref, after_ref)
        fields.append(jnp.concatenate([plane, side], axis=1))
    u, v, s1, s2, s12, strength, a, b, cx, cy = fields
    for _ in range(SUBCYCLES):
        ue, un, ve, vn = east(u), north(u), east(v), north(v)
        divergence, tension, shearing = ue + vn, ue - vn, un + ve
        square = (
            divergence * divergence
            + (tension * tension + shearing * shearing) * 0.25
            + STRAIN_FLOOR
        )
        inverse = lax.rsqrt(square)
        pull = strength * inverse
        s1 = (s1 + 0.5 * pull * (divergence - square * inverse)) * THIRD
        s2 = (s2 + 0.125 * pull * tension) * THIRD
        s12 = (s12 + 0.0625 * pull * shearing) * THIRD
        n11, n22 = 0.5 * (s1 + s2), 0.5 * (s1 - s2)
        u = a * u + b * (east(n11) + north(s12)) + cx
        v = a * v + b * (east(s12) + north(n22)) + cy
    velocity_out[0] = u[:rows, :cols]
    velocity_out[1] = v[:rows, :cols]
    stress_out[0] = s1[:rows, :cols]
    stress_out[1] = s2[:rows, :cols]
    stress_out[2] = s12[:rows, :cols]


def call(kernel, outs, flops, fetch=False):
    def run(*args):
        space = pltpu.HBM if fetch else pltpu.VMEM
        scratch = []
        if fetch:
            scratch = [pltpu.VMEM(a.shape, a.dtype) for a in args[:-1]]
            scratch += [pltpu.SMEM(args[-1].shape, jnp.int32), pltpu.SemaphoreType.DMA((len(args),))]
        return pl.pallas_call(
            kernel,
            out_shape=[jax.ShapeDtypeStruct(shape, jnp.float32) for shape in outs],
            in_specs=[pl.BlockSpec(memory_space=space)] * len(args),
            out_specs=[pl.BlockSpec(memory_space=pltpu.VMEM)] * len(outs),
            scratch_shapes=scratch,
            compiler_params=pltpu.CompilerParams(vmem_limit_bytes=(60 if fetch else 8) << 20),
            cost_estimate=pl.CostEstimate(flops=flops, bytes_accessed=flops // 8, transcendentals=0),
        )(*args)

    return run


def local(
    layer_temp,
    ice_depth_per_class,
    ice_area,
    surf_temp,
    seawater_thermal_input,
    velocity,
    stress,
    wind_stress,
    current,
    land_mask,
    ice_mask,
    band_index,
):
    rows, levels, cols = layer_temp.shape
    lat_size, lon_size = lax.axis_size("lat"), lax.axis_size("lon")
    half = (PLANES, EDGE, cols)
    swap = lambda x: jnp.transpose(x, (1, 0, 2))
    temp_after, thick_after, parts, first, last = call(
        columns_kernel,
        [(levels, rows, cols), (DEPTH_CLASSES, rows, cols), (lat_size, 1, 2 * BANDS_DEV), half, half],
        4_000_000,
        fetch=True,
    )(
        swap(layer_temp), swap(ice_depth_per_class), swap(ice_area), surf_temp,
        seawater_thermal_input, velocity, stress, wind_stress, current, land_mask, ice_mask, band_index,
    )
    arrived = lax.all_to_all(parts, "lat", 0, 0, tiled=True)
    before = lax.ppermute(last, "lat", [(i, i + 1) for i in range(lat_size - 1)])
    after = lax.ppermute(first, "lat", [(i + 1, i) for i in range(lat_size - 1)])

    total = jnp.sum(arrived, axis=(0, 1))
    share = total[:BANDS_DEV] / (total[BANDS_DEV:] * float(cols * lon_size))
    share = jnp.pad(share, (0, cols - BANDS_DEV))
    spread = jnp.broadcast_to(share[None, None], (lon_size, 1, cols))
    spread, before, after = lax.optimization_barrier((spread, before, after))
    shares = lax.all_to_all(spread, "lon", 0, 0, tiled=True)

    packed = (4 * EDGE, cols)
    right, left = call(pack_kernel, [packed, packed], 500_000)(first, last, before, after)
    west = lax.ppermute(right, "lon", [(i, (i + 1) % lon_size) for i in range(lon_size)])
    onward = lax.ppermute(left, "lon", [((i + 1) % lon_size, i) for i in range(lon_size)])
    moving, stresses = call(
        subcycles_kernel, [(2, rows, cols), (3, rows, cols)], 2_000_000
    )(first, last, before, after, west, onward)
    zonal_volume = jnp.sum(shares[:, :, :BANDS_DEV], axis=(0, 1))
    return (swap(temp_after), swap(thick_after), moving, stresses, zonal_volume)


def solution(mesh):
    return jax.shard_map(
        local,
        mesh=mesh,
        in_specs=(
            P("lat", None, "lon"),
            P("lat", None, "lon"),
            P("lat", None, "lon"),
            P("lat", "lon"),
            P("lat", "lon"),
            P(None, "lat", "lon"),
            P(None, "lat", "lon"),
            P(None, "lat", "lon"),
            P(None, "lat", "lon"),
            P("lat", "lon"),
            P("lon", "lat"),
            P("lat"),
        ),
        out_specs=(
            P("lat", None, "lon"),
            P("lat", None, "lon"),
            P(None, "lat", "lon"),
            P(None, "lat", "lon"),
            P("lat"),
        ),
        check_vma=False,
    )
```

```python
import jax
import jax.numpy as jnp
from jax import lax
from jax.experimental import pallas as pl
from jax.experimental.pallas import tpu as pltpu
from jax.sharding import PartitionSpec as P

DEPTH_CLASSES = 5
VERTICAL_LEVELS = 7
SUBCYCLES = 3
SWEEPS = 2
BANDS_DEV = 4

FREEZE_POINT = -1.8
BASE_CONDUCT = 2.03
SALT_CONDUCT = 0.416
GROWTH_RATE = 0.02
STRENGTH_DECAY = 5.0
STRAIN_FLOOR = 0.0025

PLANES = 10
EDGE = 8
WIDTH = 6
THIRD = 1.0 / 1.5
SLOT = 64


def columns_step(temp, depth, surf):
    scaled = 1.0 / (depth * depth)
    half = scaled * 0.5
    guess = temp
    for sweep in range(SWEEPS):
        conduct = [BASE_CONDUCT + SALT_CONDUCT / g for g in guess]
        coupling = [scaled * conduct[0]]
        for k in range(1, VERTICAL_LEVELS):
            coupling.append(half * (conduct[k - 1] + conduct[k]))
        coupling.append(scaled * conduct[VERTICAL_LEVELS - 1])
        ratio, passed = [], []
        for k in range(VERTICAL_LEVELS):
            source = temp[k]
            divisor = 1.0 + coupling[k] + coupling[k + 1]
            if k == 0:
                source = source + coupling[0] * surf
            else:
                divisor = divisor - coupling[k] * ratio[k - 1]
                source = source + coupling[k] * passed[k - 1]
            if k == VERTICAL_LEVELS - 1:
                source = source + coupling[VERTICAL_LEVELS] * FREEZE_POINT
            inverse = 1.0 / divisor
            ratio.append(coupling[k + 1] * inverse)
            passed.append(source * inverse)
        solved = list(passed)
        for k in range(VERTICAL_LEVELS - 2, -1, -1):
            solved[k] = passed[k] + ratio[k] * solved[k + 1]
        guess = solved
    return guess


def columns_kernel(*refs):
    n = 12
    given, outs, here, sems = refs[:n], refs[n : n + 5], refs[n + 5 : n + 5 + n], refs[-1]
    copies = [pltpu.make_async_copy(a, b, sems.at[i]) for i, (a, b) in enumerate(zip(given, here))]
    for copy in copies:
        copy.start()
    for copy in copies:
        copy.wait()
    columns_body(*here, *outs)


def columns_body(
    temp_ref, depth_ref, area_ref, surf_ref, sea_ref, velocity_ref, stress_ref, wind_ref, current_ref,
    land_ref, ice_ref, band_ref, temp_out, thick_out, parts_out, first_out, last_out,
):
    rows = surf_ref.shape[0]
    depth, area = depth_ref[...], area_ref[...]

    volume = jnp.sum(area * depth, axis=0)
    coverage = jnp.sum(area, axis=0)
    a = land_ref[...].astype(jnp.float32) * THIRD
    half = 0.5 * a
    planes = (
        velocity_ref[0], velocity_ref[1], stress_ref[0], stress_ref[1], stress_ref[2],
        volume * jnp.exp(-STRENGTH_DECAY * (1.0 - coverage)),
        a, half / (1.0 + volume),
        half * (wind_ref[0] + current_ref[0]), half * (wind_ref[1] + current_ref[1]),
    )
    for f, plane in enumerate(planes):
        first_out[f] = plane[:EDGE]
        last_out[f] = plane[rows - EDGE :]

    temp = [
        jnp.stack([temp_ref[c * VERTICAL_LEVELS + k] for c in range(DEPTH_CLASSES)])
        for k in range(VERTICAL_LEVELS)
    ]
    solved = columns_step(temp, depth, surf_ref[...][None])
    bottom = solved[-1]
    regrown = (
        depth
        + GROWTH_RATE * (BASE_CONDUCT + SALT_CONDUCT / bottom) * (FREEZE_POINT - bottom) / depth
        - sea_ref[...][None]
    )
    square = (rows, rows)
    eye = lax.broadcasted_iota(jnp.int32, square, 0) == lax.broadcasted_iota(jnp.int32, square, 1)
    ice = jnp.broadcast_to(ice_ref[...].astype(jnp.float32), square)
    ice = jnp.sum(jnp.where(eye, ice, 0.0), axis=1, keepdims=True)
    ice = jnp.broadcast_to(ice, surf_ref.shape) == 1.0
    thick = [jnp.where(ice, regrown[c], depth[c]) for c in range(DEPTH_CLASSES)]
    after = area[0] * thick[0]
    for c in range(1, DEPTH_CLASSES):
        after = after + area[c] * thick[c]
    for c in range(DEPTH_CLASSES):
        thick_out[c] = thick[c]
        for k in range(VERTICAL_LEVELS):
            temp_out[c * VERTICAL_LEVELS + k] = jnp.where(ice, solved[k][c], temp[k][c])

    owners, _, entries = parts_out.shape
    total = jnp.broadcast_to(jnp.sum(after, axis=1, keepdims=True), (rows, entries))
    entry = lax.broadcasted_iota(jnp.int32, (owners, entries), 1)
    band = BANDS_DEV * lax.broadcasted_iota(jnp.int32, (owners, entries), 0) + entry % BANDS_DEV
    parts = jnp.zeros((owners, entries), jnp.float32)
    for r in range(rows):
        value = jnp.where(entry < BANDS_DEV, jnp.broadcast_to(total[r : r + 1], parts.shape), 1.0)
        parts = parts + jnp.where(band == band_ref[r], value, 0.0)
    parts_out[...] = parts[:, None, :]


def window(f, first_ref, last_ref, before_ref, after_ref):
    return jnp.concatenate([first_ref[f], last_ref[f], after_ref[f], before_ref[f]], axis=0)


def lanes_of(shape):
    return lax.broadcasted_iota(jnp.int32, shape, 1)


def pack_kernel(first_ref, last_ref, before_ref, after_ref, right_out, left_out):
    cols = right_out.shape[1]
    lanes = lanes_of(right_out.shape)
    right = jnp.zeros(right_out.shape, jnp.float32)
    left = jnp.zeros(right_out.shape, jnp.float32)
    for f in range(PLANES):
        plane = window(f, first_ref, last_ref, before_ref, after_ref)
        at = f * WIDTH
        here = (lanes >= at) & (lanes < at + WIDTH)
        right = jnp.where(here, pltpu.roll(plane, (at + WIDTH) % cols, 1), right)
        left = jnp.where(here, pltpu.roll(plane, at, 1) if at else plane, left)
    right_out[...] = right
    left_out[...] = left


def east(p):
    n = p.shape[1]
    return (pltpu.roll(p, n - 1, 1) - pltpu.roll(p, 1, 1)) * 0.5


def north(p):
    n = p.shape[0]
    return (pltpu.roll(p, n - 1, 0) - pltpu.roll(p, 1, 0)) * 0.5


def subcycles_kernel(
    first_ref, last_ref, before_ref, after_ref, west_ref, east_ref, shares_ref, velocity_out, stress_out,
    zonal_out,
):
    rows, cols = velocity_out.shape[1:]
    zonal = jnp.sum(shares_ref[...], axis=0)
    for j in range(BANDS_DEV):
        zonal_out[j] = jnp.sum(jnp.where(lanes_of(zonal.shape) == j, zonal, 0.0))
    west, onward = west_ref[...], east_ref[...]
    lanes = lanes_of(west.shape)
    fields = []
    for f in range(PLANES):
        at = f * WIDTH
        near = pltpu.roll(onward, cols - at, 1) if at else onward
        far = pltpu.roll(west, cols - WIDTH - at, 1)
        side = jnp.where(lanes < WIDTH, near, jnp.where(lanes >= cols - WIDTH, far, 0.0))
        plane = window(f, first_ref, last_ref, before_ref, after_ref)
        fields.append(jnp.concatenate([plane, side], axis=1))
    u, v, s1, s2, s12, strength, a, b, cx, cy = fields
    for _ in range(SUBCYCLES):
        ue, un, ve, vn = east(u), north(u), east(v), north(v)
        divergence, tension, shearing = ue + vn, ue - vn, un + ve
        square = (
            divergence * divergence
            + (tension * tension + shearing * shearing) * 0.25
            + STRAIN_FLOOR
        )
        inverse = lax.rsqrt(square)
        pull = strength * inverse
        s1 = (s1 + 0.5 * pull * (divergence - square * inverse)) * THIRD
        s2 = (s2 + 0.125 * pull * tension) * THIRD
        s12 = (s12 + 0.0625 * pull * shearing) * THIRD
        n11, n22 = 0.5 * (s1 + s2), 0.5 * (s1 - s2)
        u = a * u + b * (east(n11) + north(s12)) + cx
        v = a * v + b * (east(s12) + north(n22)) + cy
    velocity_out[0] = u[:rows, :cols]
    velocity_out[1] = v[:rows, :cols]
    stress_out[0] = s1[:rows, :cols]
    stress_out[1] = s2[:rows, :cols]
    stress_out[2] = s12[:rows, :cols]


def call(kernel, outs, flops, fetch=False, smem_out=False):
    def run(*args):
        space = pltpu.HBM if fetch else pltpu.VMEM
        scratch, spaces = [], [pltpu.VMEM] * len(outs)
        if smem_out:
            spaces[-1] = pltpu.SMEM
        if fetch:
            scratch = [pltpu.VMEM(a.shape, a.dtype) for a in args[:-1]]
            scratch += [pltpu.SMEM(args[-1].shape, jnp.int32), pltpu.SemaphoreType.DMA((len(args),))]
        return pl.pallas_call(
            kernel,
            out_shape=[jax.ShapeDtypeStruct(shape, jnp.float32) for shape in outs],
            in_specs=[pl.BlockSpec(memory_space=space)] * len(args),
            out_specs=[pl.BlockSpec(memory_space=where) for where in spaces],
            scratch_shapes=scratch,
            compiler_params=pltpu.CompilerParams(vmem_limit_bytes=(60 if fetch else 8) << 20),
            cost_estimate=pl.CostEstimate(flops=flops, bytes_accessed=flops // 8, transcendentals=0),
        )(*args)

    return run


def local(
    layer_temp,
    ice_depth_per_class,
    ice_area,
    surf_temp,
    seawater_thermal_input,
    velocity,
    stress,
    wind_stress,
    current,
    land_mask,
    ice_mask,
    band_index,
):
    rows, levels, cols = layer_temp.shape
    lat_size, lon_size = lax.axis_size("lat"), lax.axis_size("lon")
    half = (PLANES, EDGE, cols)
    swap = lambda x: jnp.transpose(x, (1, 0, 2))
    temp_after, thick_after, parts, first, last = call(
        columns_kernel,
        [(levels, rows, cols), (DEPTH_CLASSES, rows, cols), (lat_size, 1, 2 * BANDS_DEV), half, half],
        4_000_000,
        fetch=True,
    )(
        swap(layer_temp), swap(ice_depth_per_class), swap(ice_area), surf_temp,
        seawater_thermal_input, velocity, stress, wind_stress, current, land_mask, ice_mask, band_index,
    )
    arrived = lax.all_to_all(parts, "lat", 0, 0, tiled=True)
    before = lax.ppermute(last, "lat", [(i, i + 1) for i in range(lat_size - 1)])
    after = lax.ppermute(first, "lat", [(i + 1, i) for i in range(lat_size - 1)])

    total = jnp.sum(arrived, axis=(0, 1))
    share = total[:BANDS_DEV] / (total[BANDS_DEV:] * float(cols * lon_size))
    share = jnp.pad(share, (0, SLOT - BANDS_DEV))
    spread = jnp.broadcast_to(share[None, None], (lon_size, 1, SLOT))
    shares = lax.all_to_all(spread, "lon", 0, 0, tiled=True)

    packed = (4 * EDGE, cols)
    right, left = call(pack_kernel, [packed, packed], 500000)(first, last, before, after)
    west = lax.ppermute(right, "lon", [(i, (i + 1) % lon_size) for i in range(lon_size)])
    onward = lax.ppermute(left, "lon", [((i + 1) % lon_size, i) for i in range(lon_size)])
    moving, stresses, zonal_volume = call(
        subcycles_kernel, [(2, rows, cols), (3, rows, cols), (BANDS_DEV,)], 2000000, smem_out=True
    )(first, last, before, after, west, onward, shares)
    return (swap(temp_after), swap(thick_after), moving, stresses, zonal_volume)


def solution(mesh):
    return jax.shard_map(
        local,
        mesh=mesh,
        in_specs=(
            P("lat", None, "lon"),
            P("lat", None, "lon"),
            P("lat", None, "lon"),
            P("lat", "lon"),
            P("lat", "lon"),
            P(None, "lat", "lon"),
            P(None, "lat", "lon"),
            P(None, "lat", "lon"),
            P(None, "lat", "lon"),
            P("lat", "lon"),
            P("lon", "lat"),
            P("lat"),
        ),
        out_specs=(
            P("lat", None, "lon"),
            P("lat", None, "lon"),
            P(None, "lat", "lon"),
            P(None, "lat", "lon"),
            P("lat"),
        ),
        check_vma=False,
    )
```

```python
import jax
import jax.numpy as jnp
from jax import lax
from jax.experimental import pallas as pl
from jax.experimental.pallas import tpu as pltpu
from jax.sharding import PartitionSpec as P

DEPTH_CLASSES = 5
VERTICAL_LEVELS = 7
SUBCYCLES = 3
SWEEPS = 2
BANDS_DEV = 4

FREEZE_POINT = -1.8
BASE_CONDUCT = 2.03
SALT_CONDUCT = 0.416
GROWTH_RATE = 0.02
STRENGTH_DECAY = 5.0
STRAIN_FLOOR = 0.0025

PLANES = 10
EDGE = 8
WIDTH = 6
THIRD = 1.0 / 1.5
SLOT = 128


def columns_step(temp, depth, surf):
    scaled = 1.0 / (depth * depth)
    half = scaled * 0.5
    guess = temp
    for sweep in range(SWEEPS):
        conduct = [BASE_CONDUCT + SALT_CONDUCT / g for g in guess]
        coupling = [scaled * conduct[0]]
        for k in range(1, VERTICAL_LEVELS):
            coupling.append(half * (conduct[k - 1] + conduct[k]))
        coupling.append(scaled * conduct[VERTICAL_LEVELS - 1])
        ratio, passed = [], []
        for k in range(VERTICAL_LEVELS):
            source = temp[k]
            divisor = 1.0 + coupling[k] + coupling[k + 1]
            if k == 0:
                source = source + coupling[0] * surf
            else:
                divisor = divisor - coupling[k] * ratio[k - 1]
                source = source + coupling[k] * passed[k - 1]
            if k == VERTICAL_LEVELS - 1:
                source = source + coupling[VERTICAL_LEVELS] * FREEZE_POINT
            inverse = 1.0 / divisor
            ratio.append(coupling[k + 1] * inverse)
            passed.append(source * inverse)
        solved = list(passed)
        for k in range(VERTICAL_LEVELS - 2, -1, -1):
            solved[k] = passed[k] + ratio[k] * solved[k + 1]
        guess = solved
    return guess


def columns_kernel(*refs):
    n = 12
    given, outs, here, sems = refs[:n], refs[n : n + 5], refs[n + 5 : n + 5 + n], refs[-1]
    copies = [pltpu.make_async_copy(a, b, sems.at[i]) for i, (a, b) in enumerate(zip(given, here))]
    for copy in copies:
        copy.start()
    for copy in copies:
        copy.wait()
    columns_body(*here, *outs)


def columns_body(
    temp_ref, depth_ref, area_ref, surf_ref, sea_ref, velocity_ref, stress_ref, wind_ref, current_ref,
    land_ref, ice_ref, band_ref, temp_out, thick_out, parts_out, first_out, last_out,
):
    rows = surf_ref.shape[0]
    depth, area = depth_ref[...], area_ref[...]

    volume = jnp.sum(area * depth, axis=0)
    coverage = jnp.sum(area, axis=0)
    a = land_ref[...].astype(jnp.float32) * THIRD
    half = 0.5 * a
    planes = (
        velocity_ref[0], velocity_ref[1], stress_ref[0], stress_ref[1], stress_ref[2],
        volume * jnp.exp(-STRENGTH_DECAY * (1.0 - coverage)),
        a, half / (1.0 + volume),
        half * (wind_ref[0] + current_ref[0]), half * (wind_ref[1] + current_ref[1]),
    )
    for f, plane in enumerate(planes):
        first_out[f] = plane[:EDGE]
        last_out[f] = plane[rows - EDGE :]

    temp = [
        jnp.stack([temp_ref[c * VERTICAL_LEVELS + k] for c in range(DEPTH_CLASSES)])
        for k in range(VERTICAL_LEVELS)
    ]
    solved = columns_step(temp, depth, surf_ref[...][None])
    bottom = solved[-1]
    regrown = (
        depth
        + GROWTH_RATE * (BASE_CONDUCT + SALT_CONDUCT / bottom) * (FREEZE_POINT - bottom) / depth
        - sea_ref[...][None]
    )
    square = (rows, rows)
    eye = lax.broadcasted_iota(jnp.int32, square, 0) == lax.broadcasted_iota(jnp.int32, square, 1)
    ice = jnp.broadcast_to(ice_ref[...].astype(jnp.float32), square)
    ice = jnp.sum(jnp.where(eye, ice, 0.0), axis=1, keepdims=True)
    ice = jnp.broadcast_to(ice, surf_ref.shape) == 1.0
    thick = [jnp.where(ice, regrown[c], depth[c]) for c in range(DEPTH_CLASSES)]
    after = area[0] * thick[0]
    for c in range(1, DEPTH_CLASSES):
        after = after + area[c] * thick[c]
    for c in range(DEPTH_CLASSES):
        thick_out[c] = thick[c]
        for k in range(VERTICAL_LEVELS):
            temp_out[c * VERTICAL_LEVELS + k] = jnp.where(ice, solved[k][c], temp[k][c])

    owners, _, entries = parts_out.shape
    total = jnp.broadcast_to(jnp.sum(after, axis=1, keepdims=True), (rows, entries))
    entry = lax.broadcasted_iota(jnp.int32, (owners, entries), 1)
    band = BANDS_DEV * lax.broadcasted_iota(jnp.int32, (owners, entries), 0) + entry % BANDS_DEV
    parts = jnp.zeros((owners, entries), jnp.float32)
    for r in range(rows):
        value = jnp.where(entry < BANDS_DEV, jnp.broadcast_to(total[r : r + 1], parts.shape), 1.0)
        parts = parts + jnp.where(band == band_ref[r], value, 0.0)
    parts_out[...] = parts[:, None, :]


def window(f, first_ref, last_ref, before_ref, after_ref):
    return jnp.concatenate([first_ref[f], last_ref[f], after_ref[f], before_ref[f]], axis=0)


def lanes_of(shape):
    return lax.broadcasted_iota(jnp.int32, shape, 1)


def pack_kernel(first_ref, last_ref, before_ref, after_ref, right_out, left_out):
    cols = right_out.shape[1]
    lanes = lanes_of(right_out.shape)
    right = jnp.zeros(right_out.shape, jnp.float32)
    left = jnp.zeros(right_out.shape, jnp.float32)
    for f in range(PLANES):
        plane = window(f, first_ref, last_ref, before_ref, after_ref)
        at = f * WIDTH
        here = (lanes >= at) & (lanes < at + WIDTH)
        right = jnp.where(here, pltpu.roll(plane, (at + WIDTH) % cols, 1), right)
        left = jnp.where(here, pltpu.roll(plane, at, 1) if at else plane, left)
    right_out[...] = right
    left_out[...] = left


def east(p):
    n = p.shape[1]
    return (pltpu.roll(p, n - 1, 1) - pltpu.roll(p, 1, 1)) * 0.5


def north(p):
    n = p.shape[0]
    return (pltpu.roll(p, n - 1, 0) - pltpu.roll(p, 1, 0)) * 0.5


def subcycles_kernel(
    first_ref, last_ref, before_ref, after_ref, west_ref, east_ref, velocity_out, stress_out
):
    rows, cols = velocity_out.shape[1:]
    west, onward = west_ref[...], east_ref[...]
    lanes = lanes_of(west.shape)
    fields = []
    for f in range(PLANES):
        at = f * WIDTH
        near = pltpu.roll(onward, cols - at, 1) if at else onward
        far = pltpu.roll(west, cols - WIDTH - at, 1)
        side = jnp.where(lanes < WIDTH, near, jnp.where(lanes >= cols - WIDTH, far, 0.0))
        plane = window(f, first_ref, last_ref, before_ref, after_ref)
        fields.append(jnp.concatenate([plane, side], axis=1))
    u, v, s1, s2, s12, strength, a, b, cx, cy = fields
    for _ in range(SUBCYCLES):
        ue, un, ve, vn = east(u), north(u), east(v), north(v)
        divergence, tension, shearing = ue + vn, ue - vn, un + ve
        square = (
            divergence * divergence
            + (tension * tension + shearing * shearing) * 0.25
            + STRAIN_FLOOR
        )
        inverse = lax.rsqrt(square)
        pull = strength * inverse
        s1 = (s1 + 0.5 * pull * (divergence - square * inverse)) * THIRD
        s2 = (s2 + 0.125 * pull * tension) * THIRD
        s12 = (s12 + 0.0625 * pull * shearing) * THIRD
        n11, n22 = 0.5 * (s1 + s2), 0.5 * (s1 - s2)
        u = a * u + b * (east(n11) + north(s12)) + cx
        v = a * v + b * (east(s12) + north(n22)) + cy
    velocity_out[0] = u[:rows, :cols]
    velocity_out[1] = v[:rows, :cols]
    stress_out[0] = s1[:rows, :cols]
    stress_out[1] = s2[:rows, :cols]
    stress_out[2] = s12[:rows, :cols]


def call(kernel, outs, flops, fetch=False):
    def run(*args):
        space = pltpu.HBM if fetch else pltpu.VMEM
        scratch = []
        if fetch:
            scratch = [pltpu.VMEM(a.shape, a.dtype) for a in args[:-1]]
            scratch += [pltpu.SMEM(args[-1].shape, jnp.int32), pltpu.SemaphoreType.DMA((len(args),))]
        return pl.pallas_call(
            kernel,
            out_shape=[jax.ShapeDtypeStruct(shape, jnp.float32) for shape in outs],
            in_specs=[pl.BlockSpec(memory_space=space)] * len(args),
            out_specs=[pl.BlockSpec(memory_space=pltpu.VMEM)] * len(outs),
            scratch_shapes=scratch,
            compiler_params=pltpu.CompilerParams(vmem_limit_bytes=(60 if fetch else 8) << 20),
            cost_estimate=pl.CostEstimate(flops=flops, bytes_accessed=flops // 8, transcendentals=0),
        )(*args)

    return run


def local(
    layer_temp,
    ice_depth_per_class,
    ice_area,
    surf_temp,
    seawater_thermal_input,
    velocity,
    stress,
    wind_stress,
    current,
    land_mask,
    ice_mask,
    band_index,
):
    rows, levels, cols = layer_temp.shape
    lat_size, lon_size = lax.axis_size("lat"), lax.axis_size("lon")
    half = (PLANES, EDGE, cols)
    swap = lambda x: jnp.transpose(x, (1, 0, 2))
    temp_after, thick_after, parts, first, last = call(
        columns_kernel,
        [(levels, rows, cols), (DEPTH_CLASSES, rows, cols), (lat_size, 1, 2 * BANDS_DEV), half, half],
        4_000_000,
        fetch=True,
    )(
        swap(layer_temp), swap(ice_depth_per_class), swap(ice_area), surf_temp,
        seawater_thermal_input, velocity, stress, wind_stress, current, land_mask, ice_mask, band_index,
    )
    arrived = lax.all_to_all(parts, "lat", 0, 0, tiled=True)
    before = lax.ppermute(last, "lat", [(i, i + 1) for i in range(lat_size - 1)])
    after = lax.ppermute(first, "lat", [(i + 1, i) for i in range(lat_size - 1)])

    total = jnp.sum(arrived, axis=(0, 1))
    share = total[:BANDS_DEV] / (total[BANDS_DEV:] * float(cols * lon_size))
    share = jnp.pad(share, (0, SLOT - BANDS_DEV))
    spread = jnp.broadcast_to(share[None, None], (lon_size, 1, SLOT))
    shares = lax.all_to_all(spread, "lon", 0, 0, tiled=True)

    packed = (4 * EDGE, cols)
    right, left = call(pack_kernel, [packed, packed], 200_000_000)(first, last, before, after)
    west = lax.ppermute(right, "lon", [(i, (i + 1) % lon_size) for i in range(lon_size)])
    onward = lax.ppermute(left, "lon", [((i + 1) % lon_size, i) for i in range(lon_size)])
    moving, stresses = call(
        subcycles_kernel, [(2, rows, cols), (3, rows, cols)], 2_000_000
    )(first, last, before, after, west, onward)
    zonal_volume = jnp.sum(shares[:, :, :BANDS_DEV], axis=(0, 1))
    return (swap(temp_after), swap(thick_after), moving, stresses, zonal_volume)


def solution(mesh):
    return jax.shard_map(
        local,
        mesh=mesh,
        in_specs=(
            P("lat", None, "lon"),
            P("lat", None, "lon"),
            P("lat", None, "lon"),
            P("lat", "lon"),
            P("lat", "lon"),
            P(None, "lat", "lon"),
            P(None, "lat", "lon"),
            P(None, "lat", "lon"),
            P(None, "lat", "lon"),
            P("lat", "lon"),
            P("lon", "lat"),
            P("lat"),
        ),
        out_specs=(
            P("lat", None, "lon"),
            P("lat", None, "lon"),
            P(None, "lat", "lon"),
            P(None, "lat", "lon"),
            P("lat"),
        ),
        check_vma=False,
    )
```

```python
import jax
import jax.numpy as jnp
from jax import lax
from jax.experimental import pallas as pl
from jax.experimental.pallas import tpu as pltpu
from jax.sharding import PartitionSpec as P

DEPTH_CLASSES = 5
VERTICAL_LEVELS = 7
SUBCYCLES = 3
SWEEPS = 2
BANDS_DEV = 4

FREEZE_POINT = -1.8
BASE_CONDUCT = 2.03
SALT_CONDUCT = 0.416
GROWTH_RATE = 0.02
STRENGTH_DECAY = 5.0
STRAIN_FLOOR = 0.0025

PLANES = 10
EDGE = 8
WIDTH = 6
THIRD = 1.0 / 1.5
SLOT = 64


def columns_step(temp, depth, surf):
    scaled = 1.0 / (depth * depth)
    half = scaled * 0.5
    guess = temp
    for sweep in range(SWEEPS):
        conduct = [BASE_CONDUCT + SALT_CONDUCT / g for g in guess]
        coupling = [scaled * conduct[0]]
        for k in range(1, VERTICAL_LEVELS):
            coupling.append(half * (conduct[k - 1] + conduct[k]))
        coupling.append(scaled * conduct[VERTICAL_LEVELS - 1])
        ratio, passed = [], []
        for k in range(VERTICAL_LEVELS):
            source = temp[k]
            divisor = 1.0 + coupling[k] + coupling[k + 1]
            if k == 0:
                source = source + coupling[0] * surf
            else:
                divisor = divisor - coupling[k] * ratio[k - 1]
                source = source + coupling[k] * passed[k - 1]
            if k == VERTICAL_LEVELS - 1:
                source = source + coupling[VERTICAL_LEVELS] * FREEZE_POINT
            inverse = 1.0 / divisor
            ratio.append(coupling[k + 1] * inverse)
            passed.append(source * inverse)
        solved = list(passed)
        for k in range(VERTICAL_LEVELS - 2, -1, -1):
            solved[k] = passed[k] + ratio[k] * solved[k + 1]
        guess = solved
    return guess


def columns_kernel(*refs):
    n = 12
    given, outs, here, sems = refs[:n], refs[n : n + 5], refs[n + 5 : n + 5 + n], refs[-1]
    copies = [pltpu.make_async_copy(a, b, sems.at[i]) for i, (a, b) in enumerate(zip(given, here))]
    for copy in copies:
        copy.start()
    for copy in copies:
        copy.wait()
    columns_body(*here, *outs)


def columns_body(
    temp_ref, depth_ref, area_ref, surf_ref, sea_ref, velocity_ref, stress_ref, wind_ref, current_ref,
    land_ref, ice_ref, band_ref, temp_out, thick_out, parts_out, last_out, first_out,
):
    rows = surf_ref.shape[0]
    depth, area = depth_ref[...], area_ref[...]

    volume = jnp.sum(area * depth, axis=0)
    coverage = jnp.sum(area, axis=0)
    a = land_ref[...].astype(jnp.float32) * THIRD
    half = 0.5 * a
    planes = (
        velocity_ref[0], velocity_ref[1], stress_ref[0], stress_ref[1], stress_ref[2],
        volume * jnp.exp(-STRENGTH_DECAY * (1.0 - coverage)),
        a, half / (1.0 + volume),
        half * (wind_ref[0] + current_ref[0]), half * (wind_ref[1] + current_ref[1]),
    )
    for f, plane in enumerate(planes):
        first_out[f] = plane[:EDGE]
        last_out[f] = plane[rows - EDGE :]

    temp = [
        jnp.stack([temp_ref[c * VERTICAL_LEVELS + k] for c in range(DEPTH_CLASSES)])
        for k in range(VERTICAL_LEVELS)
    ]
    solved = columns_step(temp, depth, surf_ref[...][None])
    bottom = solved[-1]
    regrown = (
        depth
        + GROWTH_RATE * (BASE_CONDUCT + SALT_CONDUCT / bottom) * (FREEZE_POINT - bottom) / depth
        - sea_ref[...][None]
    )
    square = (rows, rows)
    eye = lax.broadcasted_iota(jnp.int32, square, 0) == lax.broadcasted_iota(jnp.int32, square, 1)
    ice = jnp.broadcast_to(ice_ref[...].astype(jnp.float32), square)
    ice = jnp.sum(jnp.where(eye, ice, 0.0), axis=1, keepdims=True)
    ice = jnp.broadcast_to(ice, surf_ref.shape) == 1.0
    thick = [jnp.where(ice, regrown[c], depth[c]) for c in range(DEPTH_CLASSES)]
    after = area[0] * thick[0]
    for c in range(1, DEPTH_CLASSES):
        after = after + area[c] * thick[c]
    for c in range(DEPTH_CLASSES):
        thick_out[c] = thick[c]
        for k in range(VERTICAL_LEVELS):
            temp_out[c * VERTICAL_LEVELS + k] = jnp.where(ice, solved[k][c], temp[k][c])

    owners, _, entries = parts_out.shape
    total = jnp.broadcast_to(jnp.sum(after, axis=1, keepdims=True), (rows, entries))
    entry = lax.broadcasted_iota(jnp.int32, (owners, entries), 1)
    band = BANDS_DEV * lax.broadcasted_iota(jnp.int32, (owners, entries), 0) + entry % BANDS_DEV
    parts = jnp.zeros((owners, entries), jnp.float32)
    for r in range(rows):
        value = jnp.where(entry < BANDS_DEV, jnp.broadcast_to(total[r : r + 1], parts.shape), 1.0)
        parts = parts + jnp.where(band == band_ref[r], value, 0.0)
    parts_out[...] = parts[:, None, :]


def window(f, first_ref, last_ref, before_ref, after_ref):
    return jnp.concatenate([first_ref[f], last_ref[f], after_ref[f], before_ref[f]], axis=0)


def lanes_of(shape):
    return lax.broadcasted_iota(jnp.int32, shape, 1)


def pack_kernel(last_ref, first_ref, before_ref, after_ref, right_out, left_out):
    cols = right_out.shape[1]
    lanes = lanes_of(right_out.shape)
    right = jnp.zeros(right_out.shape, jnp.float32)
    left = jnp.zeros(right_out.shape, jnp.float32)
    for f in range(PLANES):
        plane = window(f, first_ref, last_ref, before_ref, after_ref)
        at = f * WIDTH
        here = (lanes >= at) & (lanes < at + WIDTH)
        right = jnp.where(here, pltpu.roll(plane, (at + WIDTH) % cols, 1), right)
        left = jnp.where(here, pltpu.roll(plane, at, 1) if at else plane, left)
    right_out[...] = right
    left_out[...] = left


def east(p):
    n = p.shape[1]
    return (pltpu.roll(p, n - 1, 1) - pltpu.roll(p, 1, 1)) * 0.5


def north(p):
    n = p.shape[0]
    return (pltpu.roll(p, n - 1, 0) - pltpu.roll(p, 1, 0)) * 0.5


def subcycles_kernel(
    last_ref, first_ref, before_ref, after_ref, west_ref, east_ref, shares_ref, velocity_out, stress_out,
    zonal_out,
):
    rows, cols = velocity_out.shape[1:]
    zonal = jnp.sum(shares_ref[...], axis=0)
    for j in range(BANDS_DEV):
        zonal_out[j] = jnp.sum(jnp.where(lanes_of(zonal.shape) == j, zonal, 0.0))
    west, onward = west_ref[...], east_ref[...]
    lanes = lanes_of(west.shape)
    fields = []
    for f in range(PLANES):
        at = f * WIDTH
        near = pltpu.roll(onward, cols - at, 1) if at else onward
        far = pltpu.roll(west, cols - WIDTH - at, 1)
        side = jnp.where(lanes < WIDTH, near, jnp.where(lanes >= cols - WIDTH, far, 0.0))
        plane = window(f, first_ref, last_ref, before_ref, after_ref)
        fields.append(jnp.concatenate([plane, side], axis=1))
    u, v, s1, s2, s12, strength, a, b, cx, cy = fields
    for _ in range(SUBCYCLES):
        ue, un, ve, vn = east(u), north(u), east(v), north(v)
        divergence, tension, shearing = ue + vn, ue - vn, un + ve
        square = (
            divergence * divergence
            + (tension * tension + shearing * shearing) * 0.25
            + STRAIN_FLOOR
        )
        inverse = lax.rsqrt(square)
        pull = strength * inverse
        s1 = (s1 + 0.5 * pull * (divergence - square * inverse)) * THIRD
        s2 = (s2 + 0.125 * pull * tension) * THIRD
        s12 = (s12 + 0.0625 * pull * shearing) * THIRD
        n11, n22 = 0.5 * (s1 + s2), 0.5 * (s1 - s2)
        u = a * u + b * (east(n11) + north(s12)) + cx
        v = a * v + b * (east(s12) + north(n22)) + cy
    velocity_out[0] = u[:rows, :cols]
    velocity_out[1] = v[:rows, :cols]
    stress_out[0] = s1[:rows, :cols]
    stress_out[1] = s2[:rows, :cols]
    stress_out[2] = s12[:rows, :cols]


def call(kernel, outs, flops, fetch=False, smem_out=False):
    def run(*args):
        space = pltpu.HBM if fetch else pltpu.VMEM
        scratch, spaces = [], [pltpu.VMEM] * len(outs)
        if smem_out:
            spaces[-1] = pltpu.SMEM
        if fetch:
            scratch = [pltpu.VMEM(a.shape, a.dtype) for a in args[:-1]]
            scratch += [pltpu.SMEM(args[-1].shape, jnp.int32), pltpu.SemaphoreType.DMA((len(args),))]
        return pl.pallas_call(
            kernel,
            out_shape=[jax.ShapeDtypeStruct(shape, jnp.float32) for shape in outs],
            in_specs=[pl.BlockSpec(memory_space=space)] * len(args),
            out_specs=[pl.BlockSpec(memory_space=where) for where in spaces],
            scratch_shapes=scratch,
            compiler_params=pltpu.CompilerParams(vmem_limit_bytes=(60 if fetch else 8) << 20),
            cost_estimate=pl.CostEstimate(flops=flops, bytes_accessed=flops // 8, transcendentals=0),
        )(*args)

    return run


def local(
    layer_temp,
    ice_depth_per_class,
    ice_area,
    surf_temp,
    seawater_thermal_input,
    velocity,
    stress,
    wind_stress,
    current,
    land_mask,
    ice_mask,
    band_index,
):
    rows, levels, cols = layer_temp.shape
    lat_size, lon_size = lax.axis_size("lat"), lax.axis_size("lon")
    half = (PLANES, EDGE, cols)
    swap = lambda x: jnp.transpose(x, (1, 0, 2))
    temp_after, thick_after, parts, last, first = call(
        columns_kernel,
        [(levels, rows, cols), (DEPTH_CLASSES, rows, cols), (lat_size, 1, 2 * BANDS_DEV), half, half],
        4_000_000,
        fetch=True,
    )(
        swap(layer_temp), swap(ice_depth_per_class), swap(ice_area), surf_temp,
        seawater_thermal_input, velocity, stress, wind_stress, current, land_mask, ice_mask, band_index,
    )
    arrived = lax.all_to_all(parts, "lat", 0, 0, tiled=True)
    before = lax.ppermute(last, "lat", [(i, i + 1) for i in range(lat_size - 1)])
    after = lax.ppermute(first, "lat", [(i + 1, i) for i in range(lat_size - 1)])

    total = jnp.sum(arrived, axis=(0, 1))
    share = total[:BANDS_DEV] / (total[BANDS_DEV:] * float(cols * lon_size))
    share = jnp.pad(share, (0, SLOT - BANDS_DEV))
    spread = jnp.broadcast_to(share[None, None], (lon_size, 1, SLOT))
    shares = lax.all_to_all(spread, "lon", 0, 0, tiled=True)

    packed = (4 * EDGE, cols)
    right, left = call(pack_kernel, [packed, packed], 500000)(last, first, before, after)
    west = lax.ppermute(right, "lon", [(i, (i + 1) % lon_size) for i in range(lon_size)])
    onward = lax.ppermute(left, "lon", [((i + 1) % lon_size, i) for i in range(lon_size)])
    moving, stresses, zonal_volume = call(
        subcycles_kernel, [(2, rows, cols), (3, rows, cols), (BANDS_DEV,)], 2000000, smem_out=True
    )(last, first, before, after, west, onward, shares)
    return (swap(temp_after), swap(thick_after), moving, stresses, zonal_volume)


def solution(mesh):
    return jax.shard_map(
        local,
        mesh=mesh,
        in_specs=(
            P("lat", None, "lon"),
            P("lat", None, "lon"),
            P("lat", None, "lon"),
            P("lat", "lon"),
            P("lat", "lon"),
            P(None, "lat", "lon"),
            P(None, "lat", "lon"),
            P(None, "lat", "lon"),
            P(None, "lat", "lon"),
            P("lat", "lon"),
            P("lon", "lat"),
            P("lat"),
        ),
        out_specs=(
            P("lat", None, "lon"),
            P("lat", None, "lon"),
            P(None, "lat", "lon"),
            P(None, "lat", "lon"),
            P("lat"),
        ),
        check_vma=False,
    )
```
